32 devices in a mesh: cells: 2 (over x), tp: 16 (over z, y, core).
Axes of the slice: x: 2, y: 2, z: 4, core: 2. Of those that a mesh axis runs over, the one named last changes fastest.
Arguments:
- hidden: bfloat16 [64, 8192], P(('cells', 'tp')), parts along dimension 0, may hold values from -6 to 6
- norm_gain: bfloat16 [8192], replicated, may hold values from 0.099609375 to 1.8984375
- qkv_weight: bfloat16 [8192, 10240], P(None, 'tp'), may hold values from -0.0625 to 0.0625
- out_weight: bfloat16 [8192, 8192], P('tp'), may hold values from -0.0625 to 0.0625
- key_values: bfloat16 [64, 64, 2048], P(('cells', 'tp')), parts along dimension 0, may hold values from -260 to 260
- cache_lengths: int32 [64], P(('cells', 'tp')), parts along dimension 0, may hold values from 1 to 64, as said below
- adapter_ids: int32 [2, 64], P(None, 'cells'), parts along dimension 1, may hold values from 0 to 63
- page_table: int32 [128, 16], P('cells'), parts along dimension 0, may hold values from 0 to 1023, as said below
- down_pages: bfloat16 [1024, 512, 256], P('tp'), may hold values from -0.0625 to 0.0625
- up_pages: bfloat16 [1024, 64, 1152], P('tp'), may hold values from -0.75 to 0.75
Outputs:
- final_hidden: bfloat16 [64, 8192], P(('cells', 'tp')), parts along dimension 0
The draws below stay inside these ranges and needn't reach their ends.
There are 2 independent parts, one for each index of `cells`. The reference program is written for one: setup_inputs(seed, part) draws one part's arguments, and reference() takes and returns one part's arrays. A program takes and returns all parts, laid end to end along the dimension named above; an argument that names none is the same for every part. Nothing has to cross between parts.
Inputs may be any that keep to these rules, and one draw needn't show every extreme that they name: page_table[a, p] // 64 is the index along tp of the device that holds page p of adapter a. Every slot holds one page, and every device holds exactly one page of each adapter. For each pair of devices, at most 8 adapters have their page for the second device held on the first, and some pair reaches 8. `cache_lengths`: some request has a full cache.
All inputs are finite; a program needn't handle non-finite values.
Results may differ from the reference program's by a relative error of at most 0.024.
Values may be sent and summed in bfloat16 or wider, within the bound.
No kernel may reach another device: no remote copies, remote signals or barrier semaphores. Data moves between devices by JAX's collectives and lax.ppermute only.
A program may use at most 384 MiB of HBM per device.

```python
import math
import jax
import jax.numpy as jnp
import numpy as np
from jax import lax

D = 8192
HEADS = 64
KVH = 8
HD = 128
RANK = 64
ADAPTERS = 64
STEPS = 2
CTX = 64
QKVW = 10240
ROWS = 32
CAP = 8
N_TP = 16


def draw_page_table(key, part):
    key = jax.random.fold_in(key, 11)
    ticket_key = jax.random.fold_in(key, 1)
    order_key = jax.random.fold_in(key, 2)
    slot_key = jax.random.fold_in(key, 3)
    leader = N_TP // 2
    tickets = jax.random.permutation(ticket_key, (N_TP - 1) * CAP)[:ADAPTERS - CAP]
    others = (leader + 1 + tickets // CAP) % N_TP
    offsets = jnp.concatenate([jnp.full((CAP,), leader, jnp.int32), others.astype(jnp.int32)])
    offsets = offsets[jax.random.permutation(order_key, ADAPTERS)]
    places = jax.vmap(lambda subkey: jax.random.permutation(subkey, ADAPTERS))(jax.random.split(slot_key, N_TP))
    holder = (jnp.arange(N_TP, dtype=jnp.int32)[None, :] + offsets[:, None]) % N_TP
    within = places[holder, jnp.arange(ADAPTERS, dtype=jnp.int32)[:, None]]
    return (holder * ADAPTERS + within).astype(jnp.int32)


def draw_cache_lengths(key, part):
    key = jax.random.fold_in(key, 7)
    length_key, spot_key = jax.random.split(key, 2)
    lengths = jax.random.randint(length_key, (ROWS,), 1, CTX + 1)
    spot = jax.random.randint(spot_key, (), 0, ROWS)
    return lengths.at[spot].set(CTX).astype(jnp.int32)


def draw_key_values(key, part):
    key = jax.random.fold_in(key, 5)
    base_key = jax.random.fold_in(key, 0)
    shape = (ROWS, CTX, 2 * KVH * HD)
    values = jnp.clip(jax.random.normal(base_key, shape, jnp.float32), -6.0, 6.0)
    return values.astype(jnp.bfloat16)


def touch_ends(array, key, smallest, high):
    shape = array.shape
    spot = [jax.random.randint(jax.random.fold_in(key, axis), (), 0, shape[axis]) for axis in range(len(shape))]
    array = array.at[tuple(spot)].set(smallest)
    longest = shape.index(max(shape))
    spot[longest] = (spot[longest] + 1) % shape[longest]
    return array.at[tuple(spot)].set(high)


def block_levels(stream_key, extent, shards, least, high):
    gain = 1.0
    for axis_at, parts in shards:
        heights = jax.random.uniform(jax.random.fold_in(jax.random.fold_in(stream_key, 6), axis_at), (parts,), jnp.float32, least / len(shards), high / len(shards))
        gain = gain * jnp.repeat(jnp.exp(heights), extent[axis_at] // parts).reshape((-1,) + (1,) * (len(extent) - 1 - axis_at))
    return gain


def cumulative_ranks(number_of, skew):
    weights = [(1 << 20) // math.isqrt(rank ** skew) + 1 for rank in range(1, number_of + 1)]
    deviation = 1 + sum(weights) // (1 << 30)
    return np.cumsum(np.array([max(1, weight // deviation) for weight in weights]))


def ranked_ids(own_key, dims, count, skew):
    listing = cumulative_ranks(count, skew)
    pick = jax.random.randint(jax.random.fold_in(own_key, 1), dims, 0, int(listing[count - 1]))
    rank = jnp.searchsorted(jnp.asarray(listing, jnp.int32), pick, side="right")
    return jax.random.permutation(jax.random.fold_in(own_key, 2), count)[rank].astype(jnp.int32)


def centred(key, extent, deviation, most, cuts=(), kind=jnp.bfloat16):
    values = deviation * jax.random.normal(key, extent, jnp.float32)
    if cuts:
        values = values * block_levels(key, extent, cuts, -0.22, 0.18)
    return jnp.clip(values, -most, most).astype(kind)


def setup_inputs(seed: int = 0, part: int = 0) -> dict:
    seeds = jax.random.split(jax.random.key(seed), 11)
    own_keys = jax.random.split(jax.random.fold_in(seeds[10], part), 11)
    return {
        "hidden": centred(own_keys[0], (ROWS, D), 1.0, 6.0, ((0, 16),)),
        "norm_gain": jnp.clip(1.0 + 0.18 * jax.random.normal(seeds[1], (D,), jnp.float32), 0.099609375, 1.8984375).astype(jnp.bfloat16),
        "qkv_weight": centred(seeds[2], (D, QKVW), D ** -0.5, 0.0625, ((1, 16),)),
        "out_weight": centred(seeds[3], (D, D), D ** -0.5, 0.0625, ((0, 16),)),
        "key_values": draw_key_values(jax.random.fold_in(jax.random.fold_in(seeds[10], part), 71), part),
        "cache_lengths": draw_cache_lengths(jax.random.fold_in(jax.random.fold_in(seeds[10], part), 71), part),
        "adapter_ids": touch_ends(ranked_ids(own_keys[6], (STEPS, ROWS), ADAPTERS, 2), jax.random.fold_in(own_keys[6], 3), 0, ADAPTERS - 1).astype(jnp.int32),
        "page_table": draw_page_table(jax.random.fold_in(jax.random.fold_in(seeds[10], part), 71), part),
        "down_pages": centred(seeds[8], (ADAPTERS * N_TP, D // N_TP, 4 * RANK), D ** -0.5, 0.0625, ((0, 16),)),
        "up_pages": centred(seeds[9], (ADAPTERS * N_TP, RANK, (QKVW + D) // N_TP), RANK ** -0.5, 0.75, ((0, 16),)),
    }


rope_base = 500000.0
norm_eps = 1e-05

def rotate(values, position):
    half_dim = values.shape[-1] // 2
    frequency = rope_base ** (-(jnp.arange(half_dim, dtype=jnp.float32) * 2.0) / values.shape[-1])
    angles = position.astype(jnp.float32)[:, None] * frequency[None, :]
    cosine = jnp.cos(angles)[:, None, :]
    sine_part = jnp.sin(angles)[:, None, :]
    leading = values[..., :half_dim]
    second = values[..., half_dim:]
    return jnp.concatenate([leading * cosine - second * sine_part, second * cosine + leading * sine_part], axis=-1)

def shrink_rows(inputs, matrices, chosen):

    def advance(summed, element):
        adapter_index, matrix = element
        selector = (chosen == adapter_index).astype(jnp.float32)[:, None]
        return (summed + selector * jnp.dot(inputs, matrix, preferred_element_type=jnp.float32), None)
    initial = jnp.zeros((inputs.shape[0], matrices.shape[2]), jnp.float32)
    summed, _ = lax.scan(advance, initial, (jnp.arange(matrices.shape[0], dtype=jnp.int32), matrices))
    return summed

def attend(queries, cached, lengths, fresh_keys, fresh_values):
    row_count = queries.shape[0]
    keys_old = cached[:, :, :KVH * HD].reshape(row_count, CTX, KVH, HD).astype(jnp.float32)
    values_old = cached[:, :, KVH * HD:].reshape(row_count, CTX, KVH, HD).astype(jnp.float32)
    scaling = HD ** (-0.5)
    query_wide = queries.astype(jnp.float32)
    old_scores = jnp.einsum('rgqd,rjgd->rgqj', query_wide, keys_old) * scaling
    visible = jnp.arange(CTX, dtype=jnp.int32)[None, :] < lengths[:, None]
    old_scores = jnp.where(visible[:, None, None, :], old_scores, -jnp.inf)
    new_scores = jnp.einsum('rgqd,rugd->rgqu', query_wide, fresh_keys.astype(jnp.float32)) * scaling
    scores = jnp.concatenate([old_scores, new_scores], axis=-1)
    highest = lax.optimization_barrier(jnp.max(scores, axis=-1, keepdims=True))
    exps = jnp.exp(scores - highest)
    weights = (exps / lax.optimization_barrier(jnp.sum(exps, axis=-1, keepdims=True))).astype(jnp.bfloat16)
    mixed = jnp.einsum('rgqj,rjgd->rgqd', weights[..., :CTX].astype(jnp.float32), values_old)
    mixed = mixed + jnp.einsum('rgqu,rugd->rgqd', weights[..., CTX:].astype(jnp.float32), fresh_values.astype(jnp.float32))
    return mixed.reshape(row_count, HEADS * HD).astype(jnp.bfloat16)

def reference(hidden, norm_gain, qkv_weight, out_weight, key_values, cache_lengths, adapter_ids, page_table, down_pages, up_pages):
    slice_width = D // N_TP
    qkv_slice = QKVW // N_TP
    kv_width = KVH * HD
    flat_slots = page_table.reshape(-1).astype(jnp.int32)
    down_full = jnp.take(down_pages, flat_slots, axis=0).reshape(ADAPTERS, D, 4 * RANK)
    up_all = jnp.take(up_pages, flat_slots, axis=0).reshape(ADAPTERS, N_TP, RANK, qkv_slice + slice_width)
    up_qkv = jnp.transpose(up_all[..., :qkv_slice], (0, 2, 1, 3)).reshape(ADAPTERS, RANK, QKVW)
    up_out = jnp.transpose(up_all[..., qkv_slice:], (0, 2, 1, 3)).reshape(ADAPTERS, RANK, D)
    residual = hidden
    keys_kept = []
    values_kept = []
    for decode_step in range(STEPS):
        chosen = adapter_ids[decode_step]
        widened = residual.astype(jnp.float32)
        normed = (widened * lax.rsqrt(lax.optimization_barrier(jnp.mean(widened * widened, axis=1, keepdims=True)) + norm_eps) * norm_gain.astype(jnp.float32)).astype(jnp.bfloat16)
        shrink = shrink_rows(normed, down_full[:, :, :3 * RANK], chosen).astype(jnp.bfloat16)
        adapter_terms = jnp.concatenate([shrink_rows(shrink[:, :RANK], up_qkv[:, :, :D], chosen), shrink_rows(shrink[:, RANK:2 * RANK], up_qkv[:, :, D:D + kv_width], chosen), shrink_rows(shrink[:, 2 * RANK:], up_qkv[:, :, D + kv_width:], chosen)], axis=1)
        joint = (jnp.dot(normed, qkv_weight, preferred_element_type=jnp.float32) + adapter_terms).astype(jnp.bfloat16)
        position = cache_lengths + decode_step
        queries = rotate(joint[:, :D].astype(jnp.float32).reshape(ROWS, HEADS, HD), position).astype(jnp.bfloat16)
        key_now = rotate(joint[:, D:D + kv_width].astype(jnp.float32).reshape(ROWS, KVH, HD), position).astype(jnp.bfloat16)
        keys_kept.append(key_now)
        values_kept.append(joint[:, D + kv_width:].reshape(ROWS, KVH, HD))
        attn = attend(queries.reshape(ROWS, KVH, HEADS // KVH, HD), key_values, cache_lengths, jnp.stack(keys_kept, axis=1), jnp.stack(values_kept, axis=1))
        out_shrink = shrink_rows(attn, down_full[:, :, 3 * RANK:], chosen).astype(jnp.bfloat16)
        summed = jnp.dot(attn, out_weight, preferred_element_type=jnp.float32) + shrink_rows(out_shrink, up_out, chosen)
        residual = (residual.astype(jnp.float32) + summed).astype(jnp.bfloat16)
    return residual
```

```python
import functools

import jax
import jax.numpy as jnp
from jax import lax
from jax.experimental import pallas as pl
from jax.experimental.pallas import tpu as pltpu
from jax.sharding import PartitionSpec as P

HEADS = 64
KVH = 8
HD = 128
RANK = 64
STEPS = 2
LANES = 128
CHUNK = 4
SPAN = 512
VMEM_LIMIT = 48 * 1024 * 1024

rope_base = 500000.0
norm_eps = 1e-05
BF16 = jnp.bfloat16
F32 = jnp.float32


def lane_window(first, width, total):
    if total % LANES:
        return 0, total
    low = first // LANES * LANES
    high = -(-(first + width) // LANES) * LANES
    return low, high - low


class Pages:
    def __init__(self, count, slots, pool, buffer, sems, first):
        self.chunks = (count[0] + CHUNK - 1) // CHUNK
        self.slots, self.pool, self.buffer, self.sems = slots, pool, buffer, sems
        self.first = first

    def start(self):
        width = self.buffer.shape[2]

        def begin(chunk, carry):
            for inner in range(CHUNK):
                at = chunk * CHUNK + inner
                pltpu.make_async_copy(
                    self.pool.at[self.slots[at], :, pl.ds(self.first, width)],
                    self.buffer.at[at],
                    self.sems.at[chunk],
                ).start()
            return carry

        lax.fori_loop(0, self.chunks, begin, 0)

    def each(self, step):
        def run(chunk, carry):
            base = pl.multiple_of(chunk * CHUNK, CHUNK)
            group = self.buffer.at[pl.ds(base, CHUNK)]
            pltpu.make_async_copy(group, group, self.sems.at[chunk]).wait()
            for inner in range(CHUNK):
                step(base + inner)
            return carry

        lax.fori_loop(0, self.chunks, run, 0)


def on_pages(kernel, out_shape, scalars, arrays, pool, window, name, scratch=()):
    used = scalars[1].shape[0]
    shape = (used, pool.shape[1], window[1])
    return pl.pallas_call(
        kernel,
        out_shape=out_shape,
        in_specs=[pl.BlockSpec(memory_space=pltpu.SMEM)] * len(scalars)
        + [pl.BlockSpec(memory_space=pltpu.VMEM)] * len(arrays)
        + [pl.BlockSpec(memory_space=pltpu.HBM)],
        out_specs=jax.tree.map(lambda _: pl.BlockSpec(memory_space=pltpu.VMEM), out_shape),
        scratch_shapes=[
            pltpu.VMEM(shape, pool.dtype),
            pltpu.SemaphoreType.DMA((used // CHUNK,)),
            *scratch,
        ],
        compiler_params=pltpu.CompilerParams(vmem_limit_bytes=VMEM_LIMIT),
        cost_estimate=pl.CostEstimate(
            flops=0,
            bytes_accessed=2 * used * shape[1] * shape[2],
            transcendentals=0,
        ),
        name=name,
    )(*scalars, *arrays, pool)


def put(total, columns, place, at, found, add=False):
    wanted = place == at
    for low in range(0, found.shape[1], LANES):
        wide = min(LANES, found.shape[1] - low)
        window = (slice(None), pl.ds(pl.multiple_of(columns + low, wide), wide))
        old = total[window]
        new = found[:, low : low + wide]
        total[window] = jnp.where(wanted[:, :wide], old + new if add else new, old)


def normalise(state, into, gain, normed):
    rows, width = state.shape
    squares = jnp.zeros((rows, SPAN), F32)
    for low in range(0, width, SPAN):
        widened = state[:, low : low + SPAN].astype(F32)
        squares = squares + widened * widened
    mean = jnp.sum(squares, axis=1, keepdims=True) / width
    scale = lax.rsqrt(mean + norm_eps)
    for low in range(0, width, SPAN):
        widened = state[:, low : low + SPAN].astype(F32)
        rounded = widened * scale * gain[:, low : low + SPAN].astype(F32)
        normed[into, low : low + SPAN] = rounded.astype(BF16)


def shrink_pages(pages, blocks, place, normed, partial):
    block = pages.pool.shape[1]
    partial[...] = jnp.zeros_like(partial)

    def step(at):
        column = pl.multiple_of(blocks[at] * block, block)
        found = jnp.dot(
            normed[:, pl.ds(column, block)], pages.buffer[at], preferred_element_type=F32
        )
        put(partial, 0, place[...], at, found)

    pages.each(step)


def shrink_kernel(
    count, slots, blocks, core, place, same, other, gain, pool, normed, partial, kept, buffer, sems, raw
):
    pages = Pages(count, slots, pool, buffer, sems, 0)
    pages.start()
    block = pool.shape[1]
    half = same.shape[0]
    for start, state in ((core[0], same), (1 - core[0], other)):
        into = pl.ds(pl.multiple_of(start * half, half), half)
        raw[into, :] = state[...]
        normalise(state, into, gain, normed)
    shrink_pages(pages, blocks, place, normed, partial)

    def keep(chunk, carry):
        for inner in range(CHUNK):
            at = chunk * CHUNK + inner
            column = pl.multiple_of(blocks[at] * block, block)
            put(kept, 0, place[...], at, raw[:, pl.ds(column, block)])
        return carry

    lax.fori_loop(0, pages.chunks, keep, 0)


def norm_and_shrink(count, slots, blocks, core, place, same, other, gain, pool):
    rows, width = place.shape[0], same.shape[1]
    _, block, ranks = pool.shape
    out_shape = (
        jax.ShapeDtypeStruct((rows, width), BF16),
        jax.ShapeDtypeStruct((rows, ranks), F32),
        jax.ShapeDtypeStruct((rows, block), BF16),
    )
    return on_pages(
        shrink_kernel,
        out_shape,
        [count, slots, blocks, core],
        [place, same, other, gain],
        pool,
        (0, ranks),
        "norm_and_shrink",
        [pltpu.VMEM((rows, width), BF16)],
    )


def blocks_kernel(
    count, slots, blocks, came, place, same, other, gain, pool, normed, partial, state, buffer, sems, raw
):
    pages = Pages(count, slots, pool, buffer, sems, 0)
    pages.start()
    chips, rows, block = same.shape

    def sort(chip, carry):
        for which, part in enumerate((same, other)):
            found = part[chip].astype(F32)
            for row in range(rows):
                at = pl.multiple_of(came[which * chips + chip, row] * block, block)
                raw[row : row + 1, pl.ds(at, block)] = found[row : row + 1]
        return carry

    lax.fori_loop(0, chips, sort, 0)
    state[...] = raw[...].astype(BF16)
    normalise(raw, slice(None), gain, normed)
    shrink_pages(pages, blocks, place, normed, partial)


def sort_norm_and_shrink(count, slots, blocks, came, place, same, other, gain, pool):
    chips, rows, block = same.shape
    width = 2 * chips * block
    ranks = pool.shape[2]
    out_shape = (
        jax.ShapeDtypeStruct((rows, width), BF16),
        jax.ShapeDtypeStruct((rows, ranks), F32),
        jax.ShapeDtypeStruct((rows, width), BF16),
    )
    return on_pages(
        blocks_kernel,
        out_shape,
        [count, slots, blocks, came],
        [place, same, other, gain],
        pool,
        (0, ranks),
        "sort_norm_and_shrink",
        [pltpu.VMEM((rows, width), F32)],
    )


def expand_kernel(width, limits, count, slots, blocks, place, shares, pool, terms, buffer, sems):
    pages = Pages(count, slots, pool, buffer, sems, 0)
    pages.start()
    rows = terms.shape[0]
    shrink = jnp.sum(shares[...].astype(F32), axis=0).astype(BF16)
    stacked = jnp.concatenate([shrink[:, :RANK], shrink[:, RANK:]], axis=0)
    lane = lax.broadcasted_iota(jnp.int32, (1, width), 1)
    terms[...] = jnp.zeros_like(terms)

    def step(at):
        found = jnp.dot(stacked, buffer[at, :, :width], preferred_element_type=F32)
        first = blocks[at] * width
        border = jnp.where(first < limits[0], limits[0], limits[1])
        later = (first + lane >= border) | (first >= limits[1])
        chosen = jnp.where(later, found[rows:], found[:rows])
        put(terms, 0, place[...], at, chosen)

    pages.each(step)


def expand(width, limits, count, slots, blocks, place, shares, pool):
    return on_pages(
        functools.partial(expand_kernel, width, limits),
        jax.ShapeDtypeStruct((place.shape[0], width), F32),
        [count, slots, blocks],
        [place, shares],
        pool,
        lane_window(0, width, pool.shape[2]),
        "expand_joint",
    )


def out_shrink_kernel(first, count, slots, place, picked, pool, partial, buffer, sems, total):
    pages = Pages(count, slots, pool, buffer, sems, first)
    pages.start()
    total[...] = jnp.zeros_like(total)

    def step(at):
        found = jnp.dot(picked[...], buffer[at], preferred_element_type=F32)
        put(total, 0, place[...], at, found)

    pages.each(step)
    partial[...] = total[:, total.shape[1] - RANK :]


def out_shrink_partial(count, slots, place, picked, pool):
    window = lane_window(pool.shape[2] - RANK, RANK, pool.shape[2])
    rows = picked.shape[0]
    return on_pages(
        functools.partial(out_shrink_kernel, window[0]),
        jax.ShapeDtypeStruct((rows, RANK), F32),
        [count, slots],
        [place, picked],
        pool,
        window,
        "out_shrink",
        [pltpu.VMEM((rows, window[1]), F32)],
    )


def project_kernel(
    first, count, slots, route, place, heads, picked, weight, pool, routed, partial, *scratch
):
    buffer, sems, tiles, tile_sems, total = scratch
    shards, depth, block = tiles.shape

    def tile(at):
        return pltpu.make_async_copy(
            weight.at[:, pl.ds(pl.multiple_of(at * block, block), block)],
            tiles.at[at],
            tile_sems.at[at],
        )

    def begin(at, carry):
        tile(at).start()
        return carry

    lax.fori_loop(0, shards, begin, 0)
    pages = Pages(count, slots, pool, buffer, sems, first)
    pages.start()

    def multiply(group, carry):
        for inner in range(CHUNK):
            at = group * CHUNK + inner
            tile(at).wait()
            found = jnp.dot(heads[...], tiles[at], preferred_element_type=F32)
            for row in range(found.shape[0]):
                routed[route[at, row], row : row + 1, :] = found[row : row + 1]
        return carry

    lax.fori_loop(0, shards // CHUNK, multiply, 0)
    total[...] = jnp.zeros_like(total)

    def step(at):
        found = jnp.dot(picked[...], buffer[at], preferred_element_type=F32)
        put(total, 0, place[...], at, found)

    pages.each(step)
    partial[...] = total[:, total.shape[1] - RANK :]


def project_and_shrink(count, slots, route, place, heads, picked, weight, pool):
    rows, depth = heads.shape
    shards = route.shape[0]
    block = weight.shape[1] // shards
    used = slots.shape[0]
    window = lane_window(pool.shape[2] - RANK, RANK, pool.shape[2])
    vmem, hbm = pl.BlockSpec(memory_space=pltpu.VMEM), pl.BlockSpec(memory_space=pltpu.HBM)
    return pl.pallas_call(
        functools.partial(project_kernel, window[0]),
        out_shape=(
            jax.ShapeDtypeStruct((shards, rows, block), F32),
            jax.ShapeDtypeStruct((rows, RANK), F32),
        ),
        in_specs=[pl.BlockSpec(memory_space=pltpu.SMEM)] * 3 + [vmem] * 3 + [hbm] * 2,
        out_specs=[vmem] * 2,
        scratch_shapes=[
            pltpu.VMEM((used, pool.shape[1], window[1]), pool.dtype),
            pltpu.SemaphoreType.DMA((used // CHUNK,)),
            pltpu.VMEM((shards, depth, block), weight.dtype),
            pltpu.SemaphoreType.DMA((shards,)),
            pltpu.VMEM((rows, window[1]), F32),
        ],
        compiler_params=pltpu.CompilerParams(vmem_limit_bytes=VMEM_LIMIT),
        cost_estimate=pl.CostEstimate(
            flops=2 * rows * weight.size, bytes_accessed=2 * weight.size, transcendentals=0
        ),
        name="project_and_shrink",
    )(count, slots, route, place, heads, picked, weight, pool)


def finish_kernel(first, count, slots, place, shrink, base, kept, pool, state, buffer, sems, total):
    pages = Pages(count, slots, pool, buffer, sems, first)
    pages.start()
    width = total.shape[1]
    inside = buffer.shape[2] - width
    total[...] = base[...] + kept[...].astype(F32)

    def step(at):
        found = jnp.dot(shrink[...], buffer[at, :, inside:], preferred_element_type=F32)
        put(total, 0, place[...], at, found, add=True)

    pages.each(step)
    state[...] = total[...].astype(BF16)


def finish_blocks(count, slots, place, shrink, base, kept, pool):
    rows, width = base.shape
    window = lane_window(pool.shape[2] - width, width, pool.shape[2])
    return on_pages(
        functools.partial(finish_kernel, window[0]),
        jax.ShapeDtypeStruct((rows, width), BF16),
        [count, slots],
        [place, shrink, base, kept],
        pool,
        window,
        "finish_blocks",
        [pltpu.VMEM((rows, width), F32)],
    )


def out_expand_kernel(
    first, width, count, slots, blocks, core, place, shares, base, pool, keep, sent, buffer, sems, shrink, send
):
    pages = Pages(count, slots, pool, buffer, sems, first)
    pages.start()
    half = keep.shape[0]
    inside = buffer.shape[2] - width
    shrink[...] = jnp.sum(shares[...].astype(F32), axis=0)
    mine = pl.multiple_of(core[0] * half, half)
    other = pl.multiple_of((1 - core[0]) * half, half)
    ordered = [shrink[pl.ds(start, half), :].astype(BF16) for start in (mine, other)]
    ordered = jnp.concatenate(ordered, axis=0)
    keep[...] = base[pl.ds(mine, half), :]
    send[...] = base[pl.ds(other, half), :]

    def step(at):
        found = jnp.dot(ordered, buffer[at, :, inside:], preferred_element_type=F32)
        column = blocks[at] * width
        put(keep, column, place[pl.ds(mine, half), :], at, found[:half], add=True)
        put(send, column, place[pl.ds(other, half), :], at, found[half:], add=True)

    pages.each(step)
    sent[...] = send[...].astype(BF16)


def out_expand(width, count, slots, blocks, core, place, shares, base, pool):
    rows = place.shape[0]
    half = (rows // 2, base.shape[1])
    window = lane_window(pool.shape[2] - width, width, pool.shape[2])
    return on_pages(
        functools.partial(out_expand_kernel, window[0], width),
        (jax.ShapeDtypeStruct(half, F32), jax.ShapeDtypeStruct(half, BF16)),
        [count, slots, blocks, core],
        [place, shares, base],
        pool,
        window,
        "expand_out",
        [pltpu.VMEM((rows, RANK), F32), pltpu.VMEM(half, F32)],
    )


def attend_kernel(
    from_parts, holders, wanted, lengths, joint, turn, cached, *refs
):
    older, (parts, fresh, heads, mixed) = refs[:-4], refs[-4:]
    row_count, positions = cached.shape[0], cached.shape[1]
    group = HEADS // KVH
    shards, block = parts.shape[0], parts.shape[2] // 2
    if from_parts:
        piece = joint.shape[2] // 2
        per = piece // HD
        for at in range(shards):
            base = joint[at, :, :piece].astype(F32)
            for row in range(row_count):
                terms = joint[holders[row, at], :, piece:].astype(F32)
                summed = base[row : row + 1] + terms[row : row + 1]
                for inner in range(per):
                    heads[row, at * per + inner : at * per + inner + 1, :] = summed[
                        :, inner * HD : (inner + 1) * HD
                    ]
    else:
        heads[...] = joint[...]
    scaling = HD ** (-0.5)
    column = lax.broadcasted_iota(jnp.int32, (HEADS, positions), 1)
    for row in range(row_count):
        rounded = heads[row].astype(BF16).astype(F32)
        plain = rounded[: HEADS + KVH]
        turned = plain * turn[row, 0:1, :] + pltpu.roll(plain, HD // 2, 1) * turn[row, 1:2, :]
        turned = turned.astype(BF16)
        fresh[row, 0] = turned[HEADS:].astype(F32)
        fresh[row, 1] = rounded[HEADS + KVH :]
        queries = turned[:HEADS]
        scores = jnp.concatenate(
            [
                lax.dot_general(
                    queries[g * group : (g + 1) * group],
                    cached[row, :, g * HD : (g + 1) * HD],
                    (((1,), (1,)), ((), ())),
                    preferred_element_type=F32,
                )
                for g in range(KVH)
            ],
            axis=0,
        )
        scores = jnp.where(column < lengths[row], scores * scaling, -jnp.inf)
        steps = [old[row] for old in older] + [fresh[row]]

        def spread(values):
            return jnp.concatenate(
                [jnp.broadcast_to(values[g : g + 1], (group, HD)) for g in range(KVH)], axis=0
            )

        wide = queries.astype(F32)
        extra = [
            jnp.sum(wide * spread(step[0]), axis=1, keepdims=True) * scaling for step in steps
        ]
        highest = jnp.max(scores, axis=1, keepdims=True)
        for one in extra:
            highest = jnp.maximum(highest, one)
        exps = jnp.exp(scores - highest)
        extra = [jnp.exp(one - highest) for one in extra]
        total = jnp.sum(exps, axis=1, keepdims=True)
        for one in extra:
            total = total + one
        weights = (exps / total).astype(BF16)
        result = jnp.concatenate(
            [
                jnp.dot(
                    weights[g * group : (g + 1) * group],
                    cached[row, :, (KVH + g) * HD : (KVH + g + 1) * HD],
                    preferred_element_type=F32,
                )
                for g in range(KVH)
            ],
            axis=0,
        )
        for one, step in zip(extra, steps):
            result = result + (one / total).astype(BF16).astype(F32) * spread(step[1])
        for at in range(shards):
            for inner in range(block // HD):
                head = at * (block // HD) + inner
                mixed[row, at, 0:1, inner * HD : (inner + 1) * HD] = result[head : head + 1]
    for at in range(shards):
        plain = [mixed[row, at, 0:1, :] for row in range(row_count)]
        picked = [mixed[row, wanted[row, at], 0:1, :] for row in range(row_count)]
        parts[at] = jnp.concatenate(
            [jnp.concatenate(plain, axis=0), jnp.concatenate(picked, axis=0)], axis=1
        ).astype(BF16)


def attend(from_parts, shards, block, holders, wanted, lengths, joint, turn, cached, older):
    row_count = cached.shape[0]
    vmem = pl.BlockSpec(memory_space=pltpu.VMEM)
    return pl.pallas_call(
        functools.partial(attend_kernel, from_parts),
        out_shape=(
            jax.ShapeDtypeStruct((shards, row_count, 2 * block), BF16),
            jax.ShapeDtypeStruct((row_count, 2, KVH, HD), F32),
        ),
        in_specs=[pl.BlockSpec(memory_space=pltpu.SMEM)] * 3 + [vmem] * (3 + len(older)),
        out_specs=[vmem] * 2,
        scratch_shapes=[
            pltpu.VMEM((row_count, HEADS + 2 * KVH, HD), F32),
            pltpu.VMEM((row_count, shards, 8, block), F32),
        ],
        compiler_params=pltpu.CompilerParams(vmem_limit_bytes=VMEM_LIMIT),
        cost_estimate=pl.CostEstimate(
            flops=0, bytes_accessed=2 * cached.size, transcendentals=0
        ),
        name="attend",
    )(holders, wanted, lengths, joint, turn, cached, *older)


def exchange(parts, groups=None):
    return lax.all_to_all(
        parts, "tp", split_axis=0, concat_axis=0, tiled=True, axis_index_groups=groups
    )


def body(
    hidden,
    norm_gain,
    qkv_weight,
    out_weight,
    key_values,
    cache_lengths,
    adapter_ids,
    page_table,
    down_pages,
    up_pages,
):
    shards = lax.axis_size("tp")
    me = lax.axis_index("tp")
    rows_dev, width = hidden.shape
    rows = rows_dev * shards
    qkv_slice = qkv_weight.shape[1]
    slice_width = out_weight.shape[0]
    adapters = page_table.shape[0]
    key_limit = width + KVH * HD
    chips = shards // 2
    core = me % 2
    chip = me // 2
    same_core = [[2 * at + which for at in range(chips)] for which in range(2)]

    def by_core(values, axis=0):
        shape = values.shape
        values = values.reshape(shape[:axis] + (chips, 2, rows_dev) + shape[axis + 1 :])
        return jnp.swapaxes(values, axis, axis + 1).reshape(shape)

    def by_device(values):
        values = values.reshape((2, chips, rows_dev) + values.shape[1:])
        return jnp.swapaxes(values, 0, 1).reshape((shards, rows_dev) + values.shape[3:])

    def swap_bits(values, bits):
        return lax.ppermute(values, "tp", [(at, at ^ bits) for at in range(shards)])

    def same_rows(own):
        return exchange(jnp.broadcast_to(own[None], (chips,) + own.shape), same_core)

    def scatter_rows(keep, send):
        summed = keep + swap_bits(send, 1).astype(F32)
        four = summed.reshape(chips // 4, 4, rows_dev, width)
        here = chip & 3
        total = lax.dynamic_index_in_dim(four, here, 1, keepdims=False)
        arrived = [
            swap_bits(
                lax.dynamic_index_in_dim(four, here ^ step, 1, keepdims=False).astype(BF16),
                2 * step,
            )
            for step in range(1, 4)
        ]
        for part in arrived:
            total = total + part.astype(F32)
        for bit in reversed(range(2, chips.bit_length() - 1)):
            here = (chip >> bit) & 1
            pair = total.reshape(2, -1, rows_dev, width)
            total = lax.dynamic_index_in_dim(pair, here, 0, keepdims=False)
            away = lax.dynamic_index_in_dim(pair, 1 - here, 0, keepdims=False)
            total = total + swap_bits(away.astype(BF16), 2 << bit).astype(F32)
        return total.reshape(rows_dev, width)

    def scatter_blocks(routed, extra):
        tail = extra.shape[0]

        def trade(away, bits):
            message = jnp.concatenate([away.reshape(-1, slice_width), extra], axis=0)
            arrived = swap_bits(message.astype(BF16), bits).astype(F32)
            return arrived[:-tail].reshape(away.shape), arrived[-tail:]

        arrived, more = trade(routed[chips:], 1)
        four = (routed[:chips] + arrived).reshape(chips // 4, 4, rows, slice_width)
        extra = extra + more
        here = chip & 3
        total = lax.dynamic_index_in_dim(four, here, 1, keepdims=False)
        traded = [
            trade(lax.dynamic_index_in_dim(four, here ^ step, 1, keepdims=False), 2 * step)
            for step in range(1, 4)
        ]
        for arrived, more in traded:
            total, extra = total + arrived, extra + more
        for bit in reversed(range(2, chips.bit_length() - 1)):
            here = (chip >> bit) & 1
            pair = total.reshape(2, -1, rows, slice_width)
            away = lax.dynamic_index_in_dim(pair, 1 - here, 0, keepdims=False)
            arrived, more = trade(away, 2 << bit)
            total = lax.dynamic_index_in_dim(pair, here, 0, keepdims=False) + arrived
            extra = extra + more
        return total.reshape(rows, slice_width), extra

    def to_all(partial):
        return exchange(jnp.broadcast_to(partial.astype(BF16)[None], (shards,) + partial.shape))

    device_iota = jnp.arange(shards, dtype=jnp.int32)
    adapter_iota = jnp.arange(adapters, dtype=jnp.int32)
    core_of = core.astype(jnp.int32).reshape(1)
    gain = norm_gain.reshape(1, width)

    def choose(ids):
        return (ids[:, :, None] == adapter_iota).astype(jnp.int32)

    def blocks_at(owners):
        return jnp.sum((owners[:, :, None] == device_iota) * device_iota[None, :, None], axis=1)

    owner_dev = page_table // adapters
    held_here = (owner_dev == me).astype(jnp.int32)
    block_here = jnp.sum(held_here * device_iota, axis=1)
    slot_here = jnp.sum(held_here * (page_table % adapters), axis=1)
    chosen = choose(adapter_ids)
    in_use = jnp.max(chosen, axis=1)
    rank = jnp.sum(in_use[:, None, :] * (adapter_iota[None, :] <= adapter_iota[:, None]), axis=-1) - 1
    listed = min(adapters, rows)
    named = in_use[:, None, :] * (rank[:, None, :] == jnp.arange(listed, dtype=jnp.int32)[:, None])
    count = jnp.sum(in_use, axis=1, keepdims=True)
    use_block = jnp.sum(named * block_here, axis=-1)
    slots = jnp.sum(named * slot_here, axis=-1)
    place = by_core(jnp.sum(chosen * rank[:, None, :], axis=-1), 1)
    place = jnp.broadcast_to(place[:, :, None], (STEPS, rows, LANES))
    block_of = by_core(jnp.sum(chosen[:, None] * blocks_at(owner_dev).T[:, None], axis=-1), 2)
    only_query = block_of * qkv_slice < width
    came = jnp.swapaxes(block_of[0].reshape(chips, 2, rows), 0, 1)
    came = jnp.where(core == 0, came, came[::-1]).reshape(shards, rows)
    holds = by_core(jnp.sum(chosen[0][:, :, None] * owner_dev, axis=1)).T
    route = ((holds % 2) ^ core) * chips + holds // 2

    mine = lax.dynamic_slice_in_dim(chosen, me * rows_dev, rows_dev, 1)
    holders = jnp.sum(mine[:, :, :, None] * owner_dev, axis=2)
    wanted = jnp.sum(mine[:, :, :, None] * blocks_at(owner_dev), axis=2)
    position = cache_lengths[None, :] + jnp.arange(STEPS, dtype=jnp.int32)[:, None]
    frequency = rope_base ** (-(jnp.arange(HD // 2, dtype=F32) * 2.0) / HD)
    angles = position.astype(F32)[:, :, None] * frequency
    cosine, sine = jnp.cos(angles), jnp.sin(angles)
    turn = jnp.stack(
        [
            jnp.concatenate([cosine, cosine], axis=-1),
            jnp.concatenate([-sine, sine], axis=-1),
        ],
        axis=2,
    )
    tables = [(holders[step], wanted[step], turn[step]) for step in range(STEPS)]
    tables.append((came, route))

    residual = hidden
    older = []
    from_parts = qkv_slice % LANES == 0
    for decode_step in range(STEPS):
        use = [count[decode_step], slots[decode_step]]
        blocks = use_block[decode_step]
        spot = place[decode_step]
        same = same_rows(residual)
        if decode_step == 0:
            same, tables = lax.optimization_barrier((same, tables))
            came, route = tables[-1]
        other = swap_bits(same, 1)
        if decode_step == 0:
            halves = [part.reshape(rows // 2, width) for part in (same, other)]
            normed, partial, kept = norm_and_shrink(
                *use, blocks, core_of, spot, *halves, gain, down_pages
            )
        else:
            normed, partial, state = sort_norm_and_shrink(
                *use, blocks, came, spot, same, other, gain, down_pages
            )
        kinds = partial[:, : 3 * RANK].astype(BF16)
        early = kinds[None, :, : 2 * RANK]
        late = kinds[None, :, RANK:]
        shares = exchange(jnp.where(only_query[decode_step][:, :, None], early, late))
        projected = jnp.dot(normed, qkv_weight, preferred_element_type=F32)
        terms = expand(qkv_slice, (width, key_limit), *use, blocks, spot, shares, up_pages)
        message = by_device(jnp.concatenate([projected, terms], axis=1).astype(BF16))
        arrived = exchange(message)
        holders, wanted, turn = tables[decode_step]
        if not from_parts:
            by_row = jnp.swapaxes(arrived, 0, 1).astype(F32)
            arrived = by_row[:, :, :qkv_slice] + jnp.take_along_axis(
                by_row[:, :, qkv_slice:], holders[:, :, None], axis=1
            )
            arrived = arrived.reshape(rows_dev, HEADS + 2 * KVH, HD)
        parts, fresh = attend(
            from_parts,
            shards,
            slice_width,
            holders,
            wanted,
            cache_lengths,
            arrived,
            turn,
            key_values,
            older,
        )
        older.append(fresh)
        headwise = by_core(exchange(parts).reshape(rows, 2 * slice_width))
        heads, picked = headwise[:, :slice_width], headwise[:, slice_width:]
        if decode_step < STEPS - 1:
            routed, partial = project_and_shrink(
                *use, route, spot, heads, picked, out_weight, down_pages
            )
            fold = slice_width // RANK
            partial = partial.reshape(fold, rows // fold, RANK)
            partial = jnp.swapaxes(partial, 0, 1).reshape(rows // fold, slice_width)
            base, shrink = scatter_blocks(routed, partial)
            shrink = jnp.swapaxes(shrink.reshape(rows // fold, fold, RANK), 0, 1)
            shrink = shrink.reshape(rows, RANK).astype(BF16)
            residual = finish_blocks(*use, spot, shrink, base, kept, up_pages)
        else:
            out_shares = to_all(out_shrink_partial(*use, spot, picked, down_pages))
            base = jnp.dot(heads, out_weight, preferred_element_type=F32)
            keep, send = out_expand(
                slice_width, *use, blocks, core_of, spot, out_shares, base, up_pages
            )
            own = core * (rows // 2) + chip * rows_dev
            own = lax.dynamic_slice_in_dim(state, own, rows_dev, 0)
            residual = (own.astype(F32) + scatter_rows(keep, send)).astype(BF16)
    return residual


def solution(mesh):
    in_specs = (
        P(("cells", "tp"), None),
        P(),
        P(None, "tp"),
        P("tp", None),
        P(("cells", "tp"), None, None),
        P(("cells", "tp")),
        P(None, "cells"),
        P("cells", None),
        P("tp", None, None),
        P("tp", None, None),
    )
    out_specs = P(("cells", "tp"), None)
    return jax.shard_map(body, mesh=mesh, in_specs=in_specs, out_specs=out_specs, check_vma=False)
```
